32 devices in a mesh: frag: 2 (over y), aux: 16 (over z, x, core).
Axes of the slice: x: 2, y: 2, z: 4, core: 2. Of those that a mesh axis runs over, the one named last changes fastest.
Arguments:
- blocks: bfloat16 [4096, 64, 128], P(('frag', 'aux')), parts along dimension 0, may hold values from -0.75 to 0.75
- slot_rows: int32 [4096], P(('frag', 'aux')), parts along dimension 0, may hold values from 0 to 15
- slot_shells: int32 [4096], P(('frag', 'aux')), parts along dimension 0, may hold values from 0 to 255, as said below
- shell_order: int32 [512], P('frag'), parts along dimension 0, may hold values from 0 to 255, as said below
- support: int32 [512, 2], P('frag'), parts along dimension 0, may hold values from 0 to 15
- coeffs: bfloat16 [512, 64, 128], P(('frag', 'aux')), parts along dimension 0, may hold values from -0.125 to 0.125
Outputs:
- exchange_matrix: float32 [2048, 1024], P(('frag', 'aux')), parts along dimension 0
The draws below stay inside these ranges and needn't reach their ends.
There are 2 independent parts, one for each index of `frag`. The reference program is written for one: setup_inputs(seed, part) draws one part's arguments, and reference() takes and returns one part's arrays. A program takes and returns all parts, laid end to end along the dimension named above; each array names one. Nothing has to cross between parts.
Inputs may be any that keep to these rules, and one draw needn't show every extreme that they name: A permutation of the 256 shells; the device holding row k of coeffs holds the coefficients of shell shell_order[k]. `slot_shells`: of the 128 blocks of one aux block, at most 16 have column shells whose coefficients one device holds; in every draw some device holds the column shells of exactly 16 blocks of every aux block.
All inputs are finite; a program needn't handle non-finite values.
Results may differ from the reference program's by a relative error of at most 0.00098.
Values may be sent and summed in bfloat16 or wider, within the bound.
A program may use at most 64 MiB of HBM per device.

```python
import jax
import jax.numpy as jnp
from jax import lax

SHELL = 64
NSH = 256
OBW = 64
NOB = 16
LOB = 2
AUX_DEV = 2
ROWS = 16
SLOTS = 128
CAP = 16
N_AUX = 16


def shared_layout(key):
    shell_order = jax.random.permutation(jax.random.fold_in(key, 11), NSH).astype(jnp.int32)
    hot_owner = jax.random.randint(jax.random.fold_in(key, 12), (), 0, N_AUX)
    tickets = N_AUX * CAP
    ticket_ids = jnp.arange(tickets, dtype=jnp.int32)
    score_keys = jax.random.split(jax.random.fold_in(key, 13), N_AUX)
    scores = jax.vmap(lambda k: jax.random.permutation(k, tickets).astype(jnp.int32))(score_keys)
    scores = jnp.where((ticket_ids // CAP)[None, :] == hot_owner, ticket_ids[None, :] - tickets, scores)
    chosen = jnp.argsort(scores, axis=1, stable=True)[:, :SLOTS]
    shuffle_keys = jax.random.split(jax.random.fold_in(key, 14), N_AUX)
    shuffled = jax.vmap(lambda k, row: row[jax.random.permutation(k, SLOTS)])(shuffle_keys, chosen)
    owners = shuffled // CAP
    within = jax.random.randint(jax.random.fold_in(key, 15), (N_AUX, SLOTS), 0, NSH // N_AUX)
    slot_shells = shell_order[owners * (NSH // N_AUX) + within]
    return (shell_order, slot_shells.reshape(N_AUX * SLOTS).astype(jnp.int32))


def draw_shell_order(key, part):
    return shared_layout(key)[0]


def draw_slot_shells(key, part):
    return shared_layout(key)[1]


def place_ends(array, own_key, least, top_value):
    spot = [jax.random.randint(jax.random.fold_in(own_key, axis), (), 0, length) for axis, length in enumerate(array.shape)]
    widest = array.shape.index(max(array.shape))
    next_to = spot[:widest] + [(spot[widest] + 1) % array.shape[widest]] + spot[widest + 1:]
    return array.at[tuple(spot)].set(least).at[tuple(next_to)].set(top_value)


def shard_levels(rng, dims, cuts, low, largest):
    def one(dim, blocks):
        heights = jax.random.uniform(jax.random.fold_in(jax.random.fold_in(rng, 6), dim), (blocks,), jnp.float32, low / len(cuts), largest / len(cuts))
        return jnp.repeat(jnp.exp(heights), dims[dim] // blocks).reshape((-1,) + (1,) * (len(dims) - dim - 1))

    gain = one(*cuts[0])
    for cut in cuts[1:]:
        gain = gain * one(*cut)
    return gain


def normal_values(rng, shape, spread, most, shards=(), held_as=jnp.bfloat16):
    result = spread * jax.random.normal(rng, shape, jnp.float32)
    if shards:
        result = result * shard_levels(rng, shape, shards, -0.22, 0.18)
    return jnp.clip(result, -most, most).astype(held_as)


def setup_inputs(seed: int = 0, part: int = 0) -> dict:
    seeds = jax.random.split(jax.random.key(seed), 7)
    part_splits = jax.random.split(jax.random.fold_in(seeds[6], part), 7)
    return {
        "blocks": normal_values(part_splits[0], (N_AUX * SLOTS, SHELL, AUX_DEV * SHELL), 0.125, 0.75, ((0, 16),)),
        "slot_rows": place_ends(jax.random.randint(part_splits[1], (N_AUX * SLOTS,), 0, ROWS), jax.random.fold_in(part_splits[1], 1), 0, ROWS - 1).astype(jnp.int32),
        "slot_shells": draw_slot_shells(jax.random.fold_in(jax.random.fold_in(seeds[6], part), 71), part),
        "shell_order": draw_shell_order(jax.random.fold_in(jax.random.fold_in(seeds[6], part), 71), part),
        "support": place_ends(jax.random.randint(part_splits[4], (NSH, LOB), 0, NOB), jax.random.fold_in(part_splits[4], 1), 0, NOB - 1).astype(jnp.int32),
        "coeffs": normal_values(part_splits[5], (NSH, SHELL, LOB * OBW), 0.02, 0.125, ((0, 16),)),
    }


def fitted_rows(values, row_ids, shell_ids, shell_order, support, coeffs):
    slot_count = values.shape[0]
    match = shell_order[None, :] == shell_ids[:, None]
    position = jnp.sum(jnp.where(match, jnp.arange(NSH, dtype=jnp.int32)[None, :], 0), axis=1).astype(jnp.int32)
    chosen = coeffs[position]
    half_blocks = jnp.einsum('slo,slq->soq', chosen.astype(jnp.float32), values.astype(jnp.float32)).astype(jnp.bfloat16)
    orbital_ids = support[shell_ids]
    row_hot = row_ids[:, None] == jnp.arange(ROWS, dtype=jnp.int32)[None, :]
    orbital_hot = orbital_ids[:, :, None] == jnp.arange(NOB, dtype=jnp.int32)[None, None, :]
    placement = (row_hot[:, None, :, None] & orbital_hot[:, :, None, :]).astype(jnp.bfloat16)
    placement = placement.reshape(slot_count * LOB, ROWS * NOB)
    flat_half = half_blocks.reshape(slot_count * LOB, OBW * AUX_DEV * SHELL)
    summed = jnp.dot(placement.T, flat_half, preferred_element_type=jnp.float32).astype(jnp.bfloat16)
    summed = summed.reshape(ROWS, NOB, OBW, AUX_DEV, SHELL).transpose(0, 4, 1, 2, 3)
    return summed.reshape(ROWS * SHELL, NOB * OBW * AUX_DEV)


def reference(blocks, slot_rows, slot_shells, shell_order, support, coeffs):
    per_block = blocks.reshape(N_AUX, SLOTS, SHELL, AUX_DEV * SHELL)
    rows_all = slot_rows.reshape(N_AUX, SLOTS)
    shells_all = slot_shells.reshape(N_AUX, SLOTS)

    def add_block(total, items):
        values, row_ids, shell_ids = items
        stacked = fitted_rows(values, row_ids, shell_ids, shell_order, support, coeffs)
        return total + jnp.dot(stacked, stacked.T, preferred_element_type=jnp.float32), None

    start_total = jnp.zeros((ROWS * SHELL, ROWS * SHELL), jnp.float32)
    total, unused = lax.scan(add_block, start_total, (per_block, rows_all, shells_all))
    return total
```

```python
import functools

import jax
import jax.numpy as jnp
from jax import lax
from jax.experimental import pallas as pl
from jax.experimental.pallas import tpu as pltpu
from jax.sharding import PartitionSpec as P

NOB = 16
ROWS = 16
NZ, NX, NC = 4, 2, 2
CHIPS = NZ * NX
REACH = CHIPS // 2


def device(z, x, c):
    return {"aux": (z * NX + x) * NC + c}


def here():
    me = lax.axis_index("aux")
    return me // (NX * NC), (me // NC) % NX, me % NC


def gather_kernel(own, out, local, z_recv, x_recv, m_recv, r_send, l_send, x_send, m_send):
    z, x, c = here()
    mate, across = device(z, x, 1 - c), device(z, 1 - x, c)

    keep = pltpu.make_async_copy(own, out.at[(z * NX + x) * NC + c], local)
    keep.start()
    barrier = pltpu.get_barrier_semaphore()
    pl.semaphore_signal(barrier, inc=1, device_id=mate)
    pl.semaphore_signal(barrier, inc=1, device_id=across)

    @pl.when(z > 0)
    def _():
        pl.semaphore_signal(barrier, inc=1, device_id=device(z - 1, x, c))

    @pl.when(z < NZ - 1)
    def _():
        pl.semaphore_signal(barrier, inc=1, device_id=device(z + 1, x, c))

    pl.semaphore_wait(barrier, 2 + jnp.where(z > 0, 1, 0) + jnp.where(z < NZ - 1, 1, 0))

    def copy(zz, xx, to, send, recv, first=False):
        spot = out.at[(zz * NX + xx) * NC + c]
        return pltpu.make_async_remote_copy(
            src_ref=own if first else spot, dst_ref=spot, send_sem=send, recv_sem=recv, device_id=to
        )

    def to_right(zz, first=False):
        return copy(zz, x, device(z + 1, x, c), r_send.at[zz], z_recv.at[zz], first)

    def to_left(zz, first=False):
        return copy(zz, x, device(z - 1, x, c), l_send.at[zz], z_recv.at[zz], first)

    def to_across(zz, first=False):
        return copy(zz, x, across, x_send.at[zz], x_recv.at[zz], first)

    def to_mate(zz, xx, first=False):
        spot = xx * NZ + zz
        return copy(zz, xx, mate, m_send.at[spot], m_recv.at[spot], first)

    def arrived_across(zz):
        pltpu.make_async_remote_copy(
            src_ref=own,
            dst_ref=out.at[(zz * NX + 1 - x) * NC + c],
            send_sem=x_send.at[zz],
            recv_sem=x_recv.at[zz],
            device_id=across,
        ).wait_recv()
        to_mate(zz, 1 - x).start()

    @pl.when(z < NZ - 1)
    def _():
        to_right(z, True).start()

    @pl.when(z > 0)
    def _():
        to_left(z, True).start()

    to_across(z, True).start()
    to_mate(z, x, True).start()
    for step in range(1, NZ):

        @pl.when(z - step >= 0)
        def _():
            zz = z - step
            copy(zz, x, across, r_send.at[zz], z_recv.at[zz]).wait_recv()

            @pl.when(z < NZ - 1)
            def _():
                to_right(zz).start()

            to_across(zz).start()
            to_mate(zz, x).start()

        @pl.when(z + step < NZ)
        def _():
            zz = z + step
            copy(zz, x, across, l_send.at[zz], z_recv.at[zz]).wait_recv()

            @pl.when(z > 0)
            def _():
                to_left(zz).start()

            to_across(zz).start()
            to_mate(zz, x).start()

        if step == 1:
            arrived_across(z)

    for step in range(1, NZ):

        @pl.when(z - step >= 0)
        def _():
            arrived_across(z - step)

        @pl.when(z + step < NZ)
        def _():
            arrived_across(z + step)

    keep.wait()
    for zz in range(NZ):

        @pl.when((zz <= z) & (z < NZ - 1))
        def _():
            to_right(zz).wait_send()

        @pl.when((zz >= z) & (z > 0))
        def _():
            to_left(zz).wait_send()

        to_across(zz).wait_send()
        for xx in range(NX):
            to_mate(zz, xx).wait_send()
            pltpu.make_async_remote_copy(
                src_ref=own,
                dst_ref=out.at[(zz * NX + xx) * NC + 1 - c],
                send_sem=m_send.at[xx * NZ + zz],
                recv_sem=m_recv.at[xx * NZ + zz],
                device_id=mate,
            ).wait_recv()


def gather_coeffs(coeffs):
    count = NZ * NX * NC
    dma = pltpu.SemaphoreType.DMA
    out = pl.pallas_call(
        gather_kernel,
        out_shape=jax.ShapeDtypeStruct((count,) + coeffs.shape, coeffs.dtype),
        in_specs=[pl.BlockSpec(memory_space=pl.ANY)],
        out_specs=pl.BlockSpec(memory_space=pl.ANY),
        scratch_shapes=[
            dma,
            dma((NZ,)),
            dma((NZ,)),
            dma((CHIPS,)),
            dma((NZ,)),
            dma((NZ,)),
            dma((NZ,)),
            dma((CHIPS,)),
        ],
        compiler_params=pltpu.CompilerParams(collective_id=0, has_side_effects=True),
        name="gather_coeffs",
    )(coeffs)
    return out.reshape((count * coeffs.shape[0],) + coeffs.shape[1:])


def fit_kernel(window, order, supp, rows, shells, coef, blocks, out, inv, acc, fit):
    shell_total = order.shape[0]
    slot_count, size, width = blocks.shape
    supp_count = supp.shape[0] // shell_total
    orb = coef.shape[2] // supp_count
    lanes = out.shape[1]
    tiles = ROWS * size // lanes
    depth = NOB * orb

    def invert(k, carry):
        inv[order[k]] = k
        return carry

    lax.fori_loop(0, shell_total, invert, 0, unroll=8)

    def clear(k, carry):
        acc[k] = jnp.zeros(acc.shape[1:], jnp.float32)
        return carry

    lax.fori_loop(0, ROWS * NOB, clear, 0, unroll=4)

    def slot(s, carry):
        shell = shells[s]
        row = rows[s]
        half = lax.dot_general(
            coef[inv[shell]], blocks[s], (((0,), (0,)), ((), ())), preferred_element_type=jnp.float32
        )
        half = half.astype(jnp.bfloat16).astype(jnp.float32)
        for a in range(supp_count):
            spot = row * NOB + supp[shell * supp_count + a]
            acc[spot] = acc[spot] + half[a * orb : (a + 1) * orb]
        return carry

    lax.fori_loop(0, slot_count, slot, 0, unroll=8)

    low = lax.broadcasted_iota(jnp.int32, (orb, width), 1) < size

    def regroup(b, carry):
        for j in range(tiles):
            even = acc[2 * j * NOB + b]
            odd = acc[(2 * j + 1) * NOB + b]
            first = jnp.where(low, even, pltpu.roll(odd, size, 1)).astype(jnp.bfloat16)
            second = jnp.where(low, pltpu.roll(even, size, 1), odd).astype(jnp.bfloat16)
            for col in range(j, fit.shape[1] // lanes, tiles):
                at = pl.ds(pl.multiple_of(b * orb, orb), orb)
                fit[at, col * lanes : (col + 1) * lanes] = first
                at = pl.ds(pl.multiple_of(depth + b * orb, orb), orb)
                fit[at, col * lanes : (col + 1) * lanes] = second
        return carry

    lax.fori_loop(0, NOB, regroup, 0)

    def multiply(i, carry):
        start = pl.multiple_of(i * lanes, lanes)
        right = fit[:, pl.ds(start, window)] if window < ROWS * size else fit[...]
        out[i] = lax.dot_general(
            fit[:, pl.ds(start, lanes)], right, (((0,), (0,)), ((), ())), preferred_element_type=jnp.float32
        )
        return carry

    lax.fori_loop(0, tiles, multiply, 0)


def fit_and_multiply(order, supp, rows, shells, coef, blocks, window):
    slot_count, size, width = blocks.shape
    orb = coef.shape[2] * order.shape[0] // supp.shape[0]
    full = ROWS * size
    held = full if window == full else full + window - width
    smem = pl.BlockSpec(memory_space=pltpu.SMEM)
    vmem = pl.BlockSpec(memory_space=pltpu.VMEM)
    return pl.pallas_call(
        functools.partial(fit_kernel, window),
        out_shape=jax.ShapeDtypeStruct((full // width, width, window), jnp.float32),
        in_specs=[smem] * 4 + [vmem] * 2,
        out_specs=vmem,
        scratch_shapes=[
            pltpu.SMEM(order.shape, jnp.int32),
            pltpu.VMEM((ROWS * NOB, orb, width), jnp.float32),
            pltpu.VMEM((NOB * orb * width // size, held), jnp.bfloat16),
        ],
        compiler_params=pltpu.CompilerParams(vmem_limit_bytes=48 * 2**20),
        name="fit_and_multiply",
    )(order, supp, rows, shells, coef, blocks)


def scatter_kernel(
    parts, out, mine, from_mate, from_across, from_line, mirror, total,
    local, m_send, m_recv, x_send, x_recv, z_send, z_recv, t_send, t_recv,
):
    z, x, c = here()
    chip = z * NX + x
    mate, across = device(z, x, 1 - c), device(z, 1 - x, c)

    def target(j):
        zz = (z + 1 + j % NZ) % NZ
        return zz * NX + (1 - x if j < NZ else x)

    keeps = []
    for j in range(CHIPS):
        keeps.append(pltpu.make_async_copy(parts.at[target(j) * NC + c], mine.at[j], local.at[j]))
        keeps[-1].start()

    barrier = pltpu.get_barrier_semaphore()
    me = lax.axis_index("aux")
    count = CHIPS * NC
    for step in range(1, count):
        pl.semaphore_signal(barrier, inc=1, device_id={"aux": lax.rem(me + step, count)})
    pl.semaphore_wait(barrier, count - 1)

    def send(src, dst, to, send_sem, recv_sem):
        copy = pltpu.make_async_remote_copy(
            src_ref=src, dst_ref=dst, send_sem=send_sem, recv_sem=recv_sem, device_id=to
        )
        copy.start()
        return copy

    to_mate = [
        send(parts.at[target(j) * NC + 1 - c], from_mate.at[j], mate, m_send.at[j], m_recv.at[j])
        for j in range(CHIPS)
    ]
    to_across = []
    for j in range(NZ):
        keeps[j].wait()
        to_mate[j].wait_recv()
        mine[j] = mine[j] + from_mate[j]
        to_across.append(send(mine.at[j], from_across.at[j], across, x_send.at[j], x_recv.at[j]))
    to_line = []
    for j in range(NZ):
        k = NZ + j
        keeps[k].wait()
        to_mate[k].wait_recv()
        mine[k] = mine[k] + from_mate[k]
    for j in range(NZ):
        k = NZ + j
        to_across[j].wait_recv()
        mine[k] = mine[k] + from_across[j]
        if j < NZ - 1:
            to_line.append(
                send(
                    mine.at[k],
                    from_line.at[j],
                    device(lax.rem(z + 1 + j, NZ), x, c),
                    z_send.at[j],
                    z_recv.at[j],
                )
            )
    for copy in to_line:
        copy.wait_recv()
    lanes = mirror.shape[3]
    for k in range(REACH + 1):
        cut = slice(k * lanes, (k + 1) * lanes)
        summed = mine[CHIPS - 1, :, cut]
        for j in range(NZ - 1):
            summed = summed + from_line[j, :, cut]
        total[k] = summed
    to_mirror = []
    for k in range(1, REACH):
        for e in range(NC):
            to_mirror.append(
                send(
                    total.at[k],
                    mirror.at[k - 1, c],
                    {"aux": lax.rem(chip + k, CHIPS) * NC + e},
                    t_send.at[k - 1, e],
                    t_recv.at[k - 1, c],
                )
            )
    for k in range(REACH + 1):
        at = pl.multiple_of(lax.rem(chip + k, CHIPS) * lanes, lanes)
        out[:, pl.ds(at, lanes)] = total[k]
    rows = out.shape[0]
    for k in range(1, REACH):
        for e in range(NC):
            pltpu.make_async_remote_copy(
                src_ref=total.at[k],
                dst_ref=mirror.at[k - 1, e],
                send_sem=t_send.at[k - 1, e],
                recv_sem=t_recv.at[k - 1, e],
                device_id=mate,
            ).wait_recv()
        turned = mirror[k - 1].reshape(NC * rows, lanes).T
        at = pl.multiple_of(lax.rem(chip + CHIPS - k, CHIPS) * lanes, lanes)
        out[:, pl.ds(at, lanes)] = jnp.where(c == 0, turned[:rows], turned[rows:])
    for copy in to_mate + to_across + to_line + to_mirror:
        copy.wait_send()


def scatter_sum(parts):
    tiles, lanes, window = parts.shape
    rows = lanes // NC
    parts = parts.reshape(tiles * NC, rows, window)
    dma = pltpu.SemaphoreType.DMA
    return pl.pallas_call(
        scatter_kernel,
        out_shape=jax.ShapeDtypeStruct((rows, tiles * lanes), jnp.float32),
        in_specs=[pl.BlockSpec(memory_space=pl.ANY)],
        out_specs=pl.BlockSpec(memory_space=pltpu.VMEM),
        scratch_shapes=[
            pltpu.VMEM((CHIPS, rows, window), jnp.float32),
            pltpu.VMEM((CHIPS, rows, window), jnp.float32),
            pltpu.VMEM((NZ, rows, window), jnp.float32),
            pltpu.VMEM((NZ - 1, rows, window), jnp.float32),
            pltpu.VMEM((REACH - 1, NC, rows, lanes), jnp.float32),
            pltpu.VMEM((REACH + 1, rows, lanes), jnp.float32),
            dma((CHIPS,)),
            dma((CHIPS,)),
            dma((CHIPS,)),
            dma((NZ,)),
            dma((NZ,)),
            dma((NZ - 1,)),
            dma((NZ - 1,)),
            dma((REACH - 1, NC)),
            dma((REACH - 1, NC)),
        ],
        compiler_params=pltpu.CompilerParams(
            collective_id=1, has_side_effects=True, vmem_limit_bytes=32 * 2**20
        ),
        name="scatter_sum",
    )(parts)


def body(near, blocks, slot_rows, slot_shells, shell_order, support, coeffs):
    full = ROWS * blocks.shape[1]
    supp = support.reshape(-1)
    if near:
        gathered = gather_coeffs(coeffs)
        window = (REACH + 1) * full // CHIPS
        parts = fit_and_multiply(shell_order, supp, slot_rows, slot_shells, gathered, blocks, window)
        return scatter_sum(parts)
    gathered = lax.all_gather(coeffs, "aux", axis=0, tiled=True)
    product = fit_and_multiply(shell_order, supp, slot_rows, slot_shells, gathered, blocks, full)
    return lax.psum_scatter(product.reshape(full, full), "aux", scatter_dimension=0, tiled=True)


def solution(mesh):
    return jax.shard_map(
        functools.partial(body, mesh.shape["aux"] == NZ * NX * NC),
        mesh=mesh,
        in_specs=(
            P(("frag", "aux"), None, None),
            P(("frag", "aux")),
            P(("frag", "aux")),
            P("frag"),
            P("frag", None),
            P(("frag", "aux"), None, None),
        ),
        out_specs=P(("frag", "aux"), None),
        check_vma=False,
    )
```

```python
import functools

import jax
import jax.numpy as jnp
from jax import lax
from jax.experimental import pallas as pl
from jax.experimental.pallas import tpu as pltpu
from jax.sharding import PartitionSpec as P

NOB = 16
ROWS = 16
NZ, NX, NC = 4, 2, 2
CHIPS = NZ * NX
REACH = CHIPS // 2


def device(z, x, c):
    return {"aux": (z * NX + x) * NC + c}


def here():
    me = lax.axis_index("aux")
    return me // (NX * NC), (me // NC) % NX, me % NC


def gather_kernel(own, out, local, z_recv, x_recv, m_recv, r_send, l_send, x_send, m_send):
    z, x, c = here()
    mate, across = device(z, x, 1 - c), device(z, 1 - x, c)

    keep = pltpu.make_async_copy(own, out.at[(z * NX + x) * NC + c], local)
    keep.start()
    barrier = pltpu.get_barrier_semaphore()
    pl.semaphore_signal(barrier, inc=1, device_id=mate)
    pl.semaphore_signal(barrier, inc=1, device_id=across)

    @pl.when(z > 0)
    def _():
        pl.semaphore_signal(barrier, inc=1, device_id=device(z - 1, x, c))

    @pl.when(z < NZ - 1)
    def _():
        pl.semaphore_signal(barrier, inc=1, device_id=device(z + 1, x, c))

    pl.semaphore_wait(barrier, 2 + jnp.where(z > 0, 1, 0) + jnp.where(z < NZ - 1, 1, 0))

    def copy(zz, xx, to, send, recv, first=False):
        spot = out.at[(zz * NX + xx) * NC + c]
        return pltpu.make_async_remote_copy(
            src_ref=own if first else spot, dst_ref=spot, send_sem=send, recv_sem=recv, device_id=to
        )

    def to_right(zz, first=False):
        return copy(zz, x, device(z + 1, x, c), r_send.at[zz], z_recv.at[zz], first)

    def to_left(zz, first=False):
        return copy(zz, x, device(z - 1, x, c), l_send.at[zz], z_recv.at[zz], first)

    def to_across(zz, first=False):
        return copy(zz, x, across, x_send.at[zz], x_recv.at[zz], first)

    def to_mate(zz, xx, first=False):
        spot = xx * NZ + zz
        return copy(zz, xx, mate, m_send.at[spot], m_recv.at[spot], first)

    def arrived_across(zz):
        pltpu.make_async_remote_copy(
            src_ref=own,
            dst_ref=out.at[(zz * NX + 1 - x) * NC + c],
            send_sem=x_send.at[zz],
            recv_sem=x_recv.at[zz],
            device_id=across,
        ).wait_recv()
        to_mate(zz, 1 - x).start()

    @pl.when(z < NZ - 1)
    def _():
        to_right(z, True).start()

    @pl.when(z > 0)
    def _():
        to_left(z, True).start()

    to_across(z, True).start()
    to_mate(z, x, True).start()
    for step in range(1, NZ):

        @pl.when(z - step >= 0)
        def _():
            zz = z - step
            copy(zz, x, across, r_send.at[zz], z_recv.at[zz]).wait_recv()

            @pl.when(z < NZ - 1)
            def _():
                to_right(zz).start()

            to_across(zz).start()
            to_mate(zz, x).start()

        @pl.when(z + step < NZ)
        def _():
            zz = z + step
            copy(zz, x, across, l_send.at[zz], z_recv.at[zz]).wait_recv()

            @pl.when(z > 0)
            def _():
                to_left(zz).start()

            to_across(zz).start()
            to_mate(zz, x).start()

        if step == 1:
            arrived_across(z)

    for step in range(1, NZ):

        @pl.when(z - step >= 0)
        def _():
            arrived_across(z - step)

        @pl.when(z + step < NZ)
        def _():
            arrived_across(z + step)

    keep.wait()
    for zz in range(NZ):

        @pl.when((zz <= z) & (z < NZ - 1))
        def _():
            to_right(zz).wait_send()

        @pl.when((zz >= z) & (z > 0))
        def _():
            to_left(zz).wait_send()

        to_across(zz).wait_send()
        for xx in range(NX):
            to_mate(zz, xx).wait_send()
            pltpu.make_async_remote_copy(
                src_ref=own,
                dst_ref=out.at[(zz * NX + xx) * NC + 1 - c],
                send_sem=m_send.at[xx * NZ + zz],
                recv_sem=m_recv.at[xx * NZ + zz],
                device_id=mate,
            ).wait_recv()


def gather_coeffs(coeffs):
    count = NZ * NX * NC
    dma = pltpu.SemaphoreType.DMA
    out = pl.pallas_call(
        gather_kernel,
        out_shape=jax.ShapeDtypeStruct((count,) + coeffs.shape, coeffs.dtype),
        in_specs=[pl.BlockSpec(memory_space=pl.ANY)],
        out_specs=pl.BlockSpec(memory_space=pl.ANY),
        scratch_shapes=[
            dma,
            dma((NZ,)),
            dma((NZ,)),
            dma((CHIPS,)),
            dma((NZ,)),
            dma((NZ,)),
            dma((NZ,)),
            dma((CHIPS,)),
        ],
        compiler_params=pltpu.CompilerParams(collective_id=0, has_side_effects=True),
        name="gather_coeffs",
    )(coeffs)
    return out.reshape((count * coeffs.shape[0],) + coeffs.shape[1:])


def fit_kernel(order, supp, rows, shells, coef, blocks, fit, inv, acc):
    shell_total = order.shape[0]
    slot_count, size, width = blocks.shape
    supp_count = supp.shape[0]
    orb = coef.shape[2] // supp_count
    tiles = fit.shape[1] // width
    depth = NOB * orb

    def invert(k, carry):
        inv[order[k]] = k
        return carry

    lax.fori_loop(0, shell_total, invert, 0, unroll=8)

    def clear(k, carry):
        acc[k] = jnp.zeros(acc.shape[1:], jnp.float32)
        return carry

    lax.fori_loop(0, ROWS * NOB, clear, 0, unroll=4)

    def slot(s, carry):
        shell = shells[s]
        row = rows[s]
        half = lax.dot_general(
            coef[inv[shell]], blocks[s], (((0,), (0,)), ((), ())), preferred_element_type=jnp.float32
        )
        half = half.astype(jnp.bfloat16).astype(jnp.float32)
        for a in range(supp_count):
            spot = row * NOB + supp[a, shell]
            acc[spot] = acc[spot] + half[a * orb : (a + 1) * orb]
        return carry

    lax.fori_loop(0, slot_count, slot, 0, unroll=8)

    low = lax.broadcasted_iota(jnp.int32, (orb, width), 1) < size

    def regroup(b, carry):
        for j in range(tiles):
            even = acc[2 * j * NOB + b]
            odd = acc[(2 * j + 1) * NOB + b]
            first = jnp.where(low, even, pltpu.roll(odd, size, 1)).astype(jnp.bfloat16)
            second = jnp.where(low, pltpu.roll(even, size, 1), odd).astype(jnp.bfloat16)
            cut = slice(j * width, (j + 1) * width)
            fit[pl.ds(pl.multiple_of(b * orb, orb), orb), cut] = first
            fit[pl.ds(pl.multiple_of(depth + b * orb, orb), orb), cut] = second
        return carry

    lax.fori_loop(0, NOB, regroup, 0)


def fit_rows(order, supp, rows, shells, coef, blocks):
    size, width = blocks.shape[1:]
    orb = coef.shape[2] // supp.shape[0]
    smem = pl.BlockSpec(memory_space=pltpu.SMEM)
    vmem = pl.BlockSpec(memory_space=pltpu.VMEM)
    return pl.pallas_call(
        fit_kernel,
        out_shape=jax.ShapeDtypeStruct((NOB * orb * width // size, ROWS * size), jnp.bfloat16),
        in_specs=[smem] * 4 + [vmem] * 2,
        out_specs=vmem,
        scratch_shapes=[
            pltpu.SMEM(order.shape, jnp.int32),
            pltpu.VMEM((ROWS * NOB, orb, width), jnp.float32),
        ],
        compiler_params=pltpu.CompilerParams(vmem_limit_bytes=40 * 2**20),
        name="fit_rows",
    )(order, supp, rows, shells, coef, blocks)


def scatter_kernel(
    fit, out, held, part, mine, from_mate, from_across, from_line, mirror, total,
    local, m_send, m_recv, x_send, x_recv, z_send, z_recv, t_send, t_recv,
):
    z, x, c = here()
    chip = z * NX + x
    mate, across = device(z, x, 1 - c), device(z, 1 - x, c)
    full = fit.shape[1]
    lanes = mirror.shape[3]
    rows, window = mine.shape[1:]

    keeps = [
        pltpu.make_async_copy(fit, held.at[:, :full], local.at[0]),
        pltpu.make_async_copy(
            fit.at[:, : window - lanes], held.at[:, full : full + window - lanes], local.at[1]
        ),
    ]
    for keep in keeps:
        keep.start()

    barrier = pltpu.get_barrier_semaphore()
    me = lax.axis_index("aux")
    count = CHIPS * NC
    for step in range(1, count):
        pl.semaphore_signal(barrier, inc=1, device_id={"aux": lax.rem(me + step, count)})
    for keep in keeps:
        keep.wait()
    pl.semaphore_wait(barrier, count - 1)

    def send(src, dst, to, send_sem, recv_sem):
        copy = pltpu.make_async_remote_copy(
            src_ref=src, dst_ref=dst, send_sem=send_sem, recv_sem=recv_sem, device_id=to
        )
        copy.start()
        return copy

    own_rows = pl.ds(pl.multiple_of(c * rows, rows), rows)
    mate_rows = pl.ds(pl.multiple_of((1 - c) * rows, rows), rows)

    def to_mate(j):
        return pltpu.make_async_remote_copy(
            src_ref=part.at[j, mate_rows],
            dst_ref=from_mate.at[j],
            send_sem=m_send.at[j],
            recv_sem=m_recv.at[j],
            device_id=mate,
        )

    def to_across(j):
        return pltpu.make_async_remote_copy(
            src_ref=mine.at[j],
            dst_ref=from_across.at[j],
            send_sem=x_send.at[j],
            recv_sem=x_recv.at[j],
            device_id=across,
        )

    def packet(j, carry):
        column = jnp.where(j < NZ, 1 - x, x)
        start = pl.multiple_of((lax.rem(z + 1 + j, NZ) * NX + column) * lanes, lanes)
        part[j] = lax.dot_general(
            held[:, pl.ds(start, lanes)],
            held[:, pl.ds(start, window)],
            (((0,), (0,)), ((), ())),
            preferred_element_type=jnp.float32,
        )
        to_mate(j).start()

        @pl.when((j >= 1) & (j <= NZ))
        def _():
            to_mate(j - 1).wait_recv()
            mine[j - 1] = part[j - 1, own_rows] + from_mate[j - 1]
            to_across(j - 1).start()

        return carry

    lax.fori_loop(0, CHIPS, packet, 0)
    to_line = []
    for j in range(NZ):
        k = NZ + j
        to_mate(k).wait_recv()
        mine[k] = part[k, own_rows] + from_mate[k]
    for j in range(NZ):
        k = NZ + j
        to_across(j).wait_recv()
        mine[k] = mine[k] + from_across[j]
        if j < NZ - 1:
            to_line.append(
                send(
                    mine.at[k],
                    from_line.at[j],
                    device(lax.rem(z + 1 + j, NZ), x, c),
                    z_send.at[j],
                    z_recv.at[j],
                )
            )
    for copy in to_line:
        copy.wait_recv()
    for k in range(REACH + 1):
        cut = slice(k * lanes, (k + 1) * lanes)
        summed = mine[CHIPS - 1, :, cut]
        for j in range(NZ - 1):
            summed = summed + from_line[j, :, cut]
        total[k] = summed
    to_mirror = []
    for k in range(1, REACH):
        for e in range(NC):
            to_mirror.append(
                send(
                    total.at[k],
                    mirror.at[k - 1, c],
                    {"aux": lax.rem(chip + k, CHIPS) * NC + e},
                    t_send.at[k - 1, e],
                    t_recv.at[k - 1, c],
                )
            )
    for k in range(REACH + 1):
        at = pl.multiple_of(lax.rem(chip + k, CHIPS) * lanes, lanes)
        out[:, pl.ds(at, lanes)] = total[k]
    for k in range(1, REACH):
        for e in range(NC):
            pltpu.make_async_remote_copy(
                src_ref=total.at[k],
                dst_ref=mirror.at[k - 1, e],
                send_sem=t_send.at[k - 1, e],
                recv_sem=t_recv.at[k - 1, e],
                device_id=mate,
            ).wait_recv()
        turned = mirror[k - 1].reshape(NC * rows, lanes).T
        at = pl.multiple_of(lax.rem(chip + CHIPS - k, CHIPS) * lanes, lanes)
        out[:, pl.ds(at, lanes)] = jnp.where(c == 0, turned[:rows], turned[rows:])
    for j in range(CHIPS):
        to_mate(j).wait_send()
    for j in range(NZ):
        to_across(j).wait_send()
    for copy in to_line + to_mirror:
        copy.wait_send()


def multiply_scatter(fit):
    depth, full = fit.shape
    lanes = full // CHIPS
    rows, window = lanes // NC, (REACH + 1) * lanes
    dma = pltpu.SemaphoreType.DMA
    return pl.pallas_call(
        scatter_kernel,
        out_shape=jax.ShapeDtypeStruct((rows, full), jnp.float32),
        in_specs=[pl.BlockSpec(memory_space=pl.ANY)],
        out_specs=pl.BlockSpec(memory_space=pltpu.VMEM),
        scratch_shapes=[
            pltpu.VMEM((depth, full + window - lanes), jnp.bfloat16),
            pltpu.VMEM((CHIPS, lanes, window), jnp.float32),
            pltpu.VMEM((CHIPS, rows, window), jnp.float32),
            pltpu.VMEM((CHIPS, rows, window), jnp.float32),
            pltpu.VMEM((NZ, rows, window), jnp.float32),
            pltpu.VMEM((NZ - 1, rows, window), jnp.float32),
            pltpu.VMEM((REACH - 1, NC, rows, lanes), jnp.float32),
            pltpu.VMEM((REACH + 1, rows, lanes), jnp.float32),
            dma((2,)),
            dma((CHIPS,)),
            dma((CHIPS,)),
            dma((NZ,)),
            dma((NZ,)),
            dma((NZ - 1,)),
            dma((NZ - 1,)),
            dma((REACH - 1, NC)),
            dma((REACH - 1, NC)),
        ],
        compiler_params=pltpu.CompilerParams(
            collective_id=1, has_side_effects=True, vmem_limit_bytes=32 * 2**20
        ),
        name="multiply_scatter",
    )(fit)


def body(near, blocks, slot_rows, slot_shells, shell_order, support, coeffs):
    gathered = gather_coeffs(coeffs) if near else lax.all_gather(coeffs, "aux", axis=0, tiled=True)
    fit = fit_rows(shell_order, support.T, slot_rows, slot_shells, gathered, blocks)
    if near:
        return multiply_scatter(fit)
    product = lax.dot_general(fit, fit, (((0,), (0,)), ((), ())), preferred_element_type=jnp.float32)
    return lax.psum_scatter(product, "aux", scatter_dimension=0, tiled=True)


def solution(mesh):
    return jax.shard_map(
        functools.partial(body, mesh.shape["aux"] == NZ * NX * NC),
        mesh=mesh,
        in_specs=(
            P(("frag", "aux"), None, None),
            P(("frag", "aux")),
            P(("frag", "aux")),
            P("frag"),
            P("frag", None),
            P(("frag", "aux"), None, None),
        ),
        out_specs=P(("frag", "aux"), None),
        check_vma=False,
    )
```

```python
import functools

import jax
import jax.numpy as jnp
from jax import lax
from jax.experimental import pallas as pl
from jax.experimental.pallas import tpu as pltpu
from jax.sharding import PartitionSpec as P

NOB = 16
ROWS = 16
NZ, NX, NC = 4, 2, 2
CHIPS = NZ * NX
REACH = CHIPS // 2


def device(z, x, c):
    return {"aux": (z * NX + x) * NC + c}


def here():
    me = lax.axis_index("aux")
    return me // (NX * NC), (me // NC) % NX, me % NC


def gather_kernel(own, out, local, z_recv, x_recv, m_recv, r_send, l_send, x_send, m_send):
    z, x, c = here()
    mate, across = device(z, x, 1 - c), device(z, 1 - x, c)

    keep = pltpu.make_async_copy(own, out.at[(z * NX + x) * NC + c], local)
    keep.start()
    barrier = pltpu.get_barrier_semaphore()
    pl.semaphore_signal(barrier, inc=1, device_id=mate)
    pl.semaphore_signal(barrier, inc=1, device_id=across)

    @pl.when(z > 0)
    def _():
        pl.semaphore_signal(barrier, inc=1, device_id=device(z - 1, x, c))

    @pl.when(z < NZ - 1)
    def _():
        pl.semaphore_signal(barrier, inc=1, device_id=device(z + 1, x, c))

    pl.semaphore_wait(barrier, 2 + jnp.where(z > 0, 1, 0) + jnp.where(z < NZ - 1, 1, 0))

    def copy(zz, xx, to, send, recv, first=False):
        spot = out.at[(zz * NX + xx) * NC + c]
        return pltpu.make_async_remote_copy(
            src_ref=own if first else spot, dst_ref=spot, send_sem=send, recv_sem=recv, device_id=to
        )

    def to_right(zz, first=False):
        return copy(zz, x, device(z + 1, x, c), r_send.at[zz], z_recv.at[zz], first)

    def to_left(zz, first=False):
        return copy(zz, x, device(z - 1, x, c), l_send.at[zz], z_recv.at[zz], first)

    def to_across(zz, first=False):
        return copy(zz, x, across, x_send.at[zz], x_recv.at[zz], first)

    def to_mate(zz, xx, first=False):
        spot = xx * NZ + zz
        return copy(zz, xx, mate, m_send.at[spot], m_recv.at[spot], first)

    def arrived_across(zz):
        pltpu.make_async_remote_copy(
            src_ref=own,
            dst_ref=out.at[(zz * NX + 1 - x) * NC + c],
            send_sem=x_send.at[zz],
            recv_sem=x_recv.at[zz],
            device_id=across,
        ).wait_recv()
        to_mate(zz, 1 - x).start()

    @pl.when(z < NZ - 1)
    def _():
        to_right(z, True).start()

    @pl.when(z > 0)
    def _():
        to_left(z, True).start()

    to_across(z, True).start()
    to_mate(z, x, True).start()
    for step in range(1, NZ):

        @pl.when(z - step >= 0)
        def _():
            zz = z - step
            copy(zz, x, across, r_send.at[zz], z_recv.at[zz]).wait_recv()

            @pl.when(z < NZ - 1)
            def _():
                to_right(zz).start()

            to_across(zz).start()
            to_mate(zz, x).start()

        @pl.when(z + step < NZ)
        def _():
            zz = z + step
            copy(zz, x, across, l_send.at[zz], z_recv.at[zz]).wait_recv()

            @pl.when(z > 0)
            def _():
                to_left(zz).start()

            to_across(zz).start()
            to_mate(zz, x).start()

        if step == 1:
            arrived_across(z)

    for step in range(1, NZ):

        @pl.when(z - step >= 0)
        def _():
            arrived_across(z - step)

        @pl.when(z + step < NZ)
        def _():
            arrived_across(z + step)

    keep.wait()
    for zz in range(NZ):

        @pl.when((zz <= z) & (z < NZ - 1))
        def _():
            to_right(zz).wait_send()

        @pl.when((zz >= z) & (z > 0))
        def _():
            to_left(zz).wait_send()

        to_across(zz).wait_send()
        for xx in range(NX):
            to_mate(zz, xx).wait_send()
            pltpu.make_async_remote_copy(
                src_ref=own,
                dst_ref=out.at[(zz * NX + xx) * NC + 1 - c],
                send_sem=m_send.at[xx * NZ + zz],
                recv_sem=m_recv.at[xx * NZ + zz],
                device_id=mate,
            ).wait_recv()


def gather_coeffs(coeffs):
    count = NZ * NX * NC
    dma = pltpu.SemaphoreType.DMA
    out = pl.pallas_call(
        gather_kernel,
        out_shape=jax.ShapeDtypeStruct((count,) + coeffs.shape, coeffs.dtype),
        in_specs=[pl.BlockSpec(memory_space=pl.ANY)],
        out_specs=pl.BlockSpec(memory_space=pl.ANY),
        scratch_shapes=[
            dma,
            dma((NZ,)),
            dma((NZ,)),
            dma((CHIPS,)),
            dma((NZ,)),
            dma((NZ,)),
            dma((NZ,)),
            dma((CHIPS,)),
        ],
        compiler_params=pltpu.CompilerParams(collective_id=0, has_side_effects=True),
        name="gather_coeffs",
    )(coeffs)
    return out.reshape((count * coeffs.shape[0],) + coeffs.shape[1:])


def fit_kernel(order, supp, rows, shells, gathered, blocks, fit, inv, acc, coef, loaded):
    load = pltpu.make_async_copy(gathered, coef, loaded)
    load.start()
    shell_total = order.shape[0]
    slot_count, size, width = blocks.shape
    supp_count = supp.shape[0]
    orb = coef.shape[2] // supp_count
    tiles = fit.shape[1] // width
    depth = NOB * orb

    def invert(k, carry):
        inv[order[k]] = k
        return carry

    lax.fori_loop(0, shell_total, invert, 0, unroll=8)

    def clear(k, carry):
        acc[k] = jnp.zeros(acc.shape[1:], jnp.float32)
        return carry

    lax.fori_loop(0, ROWS * NOB, clear, 0, unroll=4)
    load.wait()

    def slot(s, carry):
        shell = shells[s]
        row = rows[s]
        half = lax.dot_general(
            coef[inv[shell]], blocks[s], (((0,), (0,)), ((), ())), preferred_element_type=jnp.float32
        )
        half = half.astype(jnp.bfloat16).astype(jnp.float32)
        for a in range(supp_count):
            spot = row * NOB + supp[a, shell]
            acc[spot] = acc[spot] + half[a * orb : (a + 1) * orb]
        return carry

    lax.fori_loop(0, slot_count, slot, 0, unroll=8)

    low = lax.broadcasted_iota(jnp.int32, (orb, width), 1) < size

    def regroup(b, carry):
        for j in range(tiles):
            even = acc[2 * j * NOB + b]
            odd = acc[(2 * j + 1) * NOB + b]
            first = jnp.where(low, even, pltpu.roll(odd, size, 1)).astype(jnp.bfloat16)
            second = jnp.where(low, pltpu.roll(even, size, 1), odd).astype(jnp.bfloat16)
            cut = slice(j * width, (j + 1) * width)
            fit[pl.ds(pl.multiple_of(b * orb, orb), orb), cut] = first
            fit[pl.ds(pl.multiple_of(depth + b * orb, orb), orb), cut] = second
        return carry

    lax.fori_loop(0, NOB, regroup, 0)


def fit_rows(order, supp, rows, shells, coef, blocks):
    size, width = blocks.shape[1:]
    orb = coef.shape[2] // supp.shape[0]
    smem = pl.BlockSpec(memory_space=pltpu.SMEM)
    vmem = pl.BlockSpec(memory_space=pltpu.VMEM)
    return pl.pallas_call(
        fit_kernel,
        out_shape=jax.ShapeDtypeStruct((NOB * orb * width // size, ROWS * size), jnp.bfloat16),
        in_specs=[smem] * 4 + [pl.BlockSpec(memory_space=pl.ANY), vmem],
        out_specs=vmem,
        scratch_shapes=[
            pltpu.SMEM(order.shape, jnp.int32),
            pltpu.VMEM((ROWS * NOB, orb, width), jnp.float32),
            pltpu.VMEM(coef.shape, coef.dtype),
            pltpu.SemaphoreType.DMA,
        ],
        compiler_params=pltpu.CompilerParams(vmem_limit_bytes=46 * 2**20),
        name="fit_rows",
    )(order, supp, rows, shells, coef, blocks)


def scatter_kernel(
    fit, out, held, part, from_mate, mine_a, mine_b, across_a, across_b, line_a, line_b, mirror, total,
    local, m_send, m_recv, x_send, x_recv, z_send, z_recv, t_send, t_recv,
):
    z, x, c = here()
    chip = z * NX + x
    mate, across = device(z, x, 1 - c), device(z, 1 - x, c)
    full = fit.shape[1]
    lanes = mirror.shape[3]
    rows, window = from_mate.shape[1:]
    mine, from_across, from_line = (mine_a, mine_b), (across_a, across_b), (line_a, line_b)

    keeps = [
        pltpu.make_async_copy(fit, held.at[:, :full], local.at[0]),
        pltpu.make_async_copy(
            fit.at[:, : window - lanes], held.at[:, full : full + window - lanes], local.at[1]
        ),
    ]
    for keep in keeps:
        keep.start()

    barrier = pltpu.get_barrier_semaphore()
    me = lax.axis_index("aux")
    count = CHIPS * NC
    for step in range(1, count):
        pl.semaphore_signal(barrier, inc=1, device_id={"aux": lax.rem(me + step, count)})
    for keep in keeps:
        keep.wait()
    pl.semaphore_wait(barrier, count - 1)

    def send(src, dst, to, send_sem, recv_sem):
        copy = pltpu.make_async_remote_copy(
            src_ref=src, dst_ref=dst, send_sem=send_sem, recv_sem=recv_sem, device_id=to
        )
        copy.start()
        return copy

    own_rows = pl.ds(pl.multiple_of(c * rows, rows), rows)
    mate_rows = pl.ds(pl.multiple_of((1 - c) * rows, rows), rows)

    def to_mate(j):
        return pltpu.make_async_remote_copy(
            src_ref=part.at[j, mate_rows],
            dst_ref=from_mate.at[j],
            send_sem=m_send.at[j],
            recv_sem=m_recv.at[j],
            device_id=mate,
        )

    def to_across(g, j):
        return pltpu.make_async_remote_copy(
            src_ref=mine[g].at[j],
            dst_ref=from_across[g].at[j],
            send_sem=x_send.at[g, j],
            recv_sem=x_recv.at[g, j],
            device_id=across,
        )

    def add_pair(j):
        to_mate(j).wait_recv()
        both = part[j, own_rows] + from_mate[j]
        mine_a[j] = both[:, lanes : REACH * lanes]
        mine_b[j, :, :lanes] = both[:, :lanes]
        mine_b[j, :, lanes:] = both[:, REACH * lanes :]

    def packet(j, carry):
        column = jnp.where(j < NZ, 1 - x, x)
        start = pl.multiple_of((lax.rem(z + 1 + j, NZ) * NX + column) * lanes, lanes)
        part[j] = lax.dot_general(
            held[:, pl.ds(start, lanes)],
            held[:, pl.ds(start, window)],
            (((0,), (0,)), ((), ())),
            preferred_element_type=jnp.float32,
        )
        to_mate(j).start()

        @pl.when((j >= 1) & (j <= NZ))
        def _():
            add_pair(j - 1)
            to_across(0, j - 1).start()

        return carry

    lax.fori_loop(0, CHIPS, packet, 0)
    to_line = []

    def pass_on(g, j):
        k = NZ + j
        to_across(g, j).wait_recv()
        mine[g][k] = mine[g][k] + from_across[g][j]
        if j < NZ - 1:
            to_line.append(
                send(
                    mine[g].at[k],
                    from_line[g].at[j],
                    device(lax.rem(z + 1 + j, NZ), x, c),
                    z_send.at[g, j],
                    z_recv.at[g, j],
                )
            )

    def finish(g, blocks):
        for copy in to_line[g * (NZ - 1) : (g + 1) * (NZ - 1)]:
            copy.wait_recv()
        for at, k in enumerate(blocks):
            cut = slice(at * lanes, (at + 1) * lanes)
            summed = mine[g][CHIPS - 1, :, cut]
            for j in range(NZ - 1):
                summed = summed + from_line[g][j, :, cut]
            total[k] = summed

    for j in range(NZ):
        add_pair(NZ + j)
    for j in range(NZ):
        pass_on(0, j)
        to_across(1, j).start()
    pass_on(1, 0)
    pass_on(1, 1)
    finish(0, range(1, REACH))
    to_mirror = []
    for k in range(1, REACH):
        for e in range(NC):
            to_mirror.append(
                send(
                    total.at[k],
                    mirror.at[k - 1, c],
                    {"aux": lax.rem(chip + k, CHIPS) * NC + e},
                    t_send.at[k - 1, e],
                    t_recv.at[k - 1, c],
                )
            )
    for j in range(2, NZ):
        pass_on(1, j)
    finish(1, (0, REACH))
    for k in range(REACH + 1):
        at = pl.multiple_of(lax.rem(chip + k, CHIPS) * lanes, lanes)
        out[:, pl.ds(at, lanes)] = total[k]
    for k in range(1, REACH):
        for e in range(NC):
            pltpu.make_async_remote_copy(
                src_ref=total.at[k],
                dst_ref=mirror.at[k - 1, e],
                send_sem=t_send.at[k - 1, e],
                recv_sem=t_recv.at[k - 1, e],
                device_id=mate,
            ).wait_recv()
        turned = mirror[k - 1].reshape(NC * rows, lanes).T
        at = pl.multiple_of(lax.rem(chip + CHIPS - k, CHIPS) * lanes, lanes)
        out[:, pl.ds(at, lanes)] = jnp.where(c == 0, turned[:rows], turned[rows:])
    for j in range(CHIPS):
        to_mate(j).wait_send()
    for g in range(2):
        for j in range(NZ):
            to_across(g, j).wait_send()
    for copy in to_line + to_mirror:
        copy.wait_send()


def multiply_scatter(fit):
    depth, full = fit.shape
    lanes = full // CHIPS
    rows, window = lanes // NC, (REACH + 1) * lanes
    first = (REACH - 1) * lanes
    dma = pltpu.SemaphoreType.DMA
    return pl.pallas_call(
        scatter_kernel,
        out_shape=jax.ShapeDtypeStruct((rows, full), jnp.float32),
        in_specs=[pl.BlockSpec(memory_space=pl.ANY)],
        out_specs=pl.BlockSpec(memory_space=pltpu.VMEM),
        scratch_shapes=[
            pltpu.VMEM((depth, full + window - lanes), jnp.bfloat16),
            pltpu.VMEM((CHIPS, lanes, window), jnp.float32),
            pltpu.VMEM((CHIPS, rows, window), jnp.float32),
            pltpu.VMEM((CHIPS, rows, first), jnp.float32),
            pltpu.VMEM((CHIPS, rows, window - first), jnp.float32),
            pltpu.VMEM((NZ, rows, first), jnp.float32),
            pltpu.VMEM((NZ, rows, window - first), jnp.float32),
            pltpu.VMEM((NZ - 1, rows, first), jnp.float32),
            pltpu.VMEM((NZ - 1, rows, window - first), jnp.float32),
            pltpu.VMEM((REACH - 1, NC, rows, lanes), jnp.float32),
            pltpu.VMEM((REACH + 1, rows, lanes), jnp.float32),
            dma((2,)),
            dma((CHIPS,)),
            dma((CHIPS,)),
            dma((2, NZ)),
            dma((2, NZ)),
            dma((2, NZ - 1)),
            dma((2, NZ - 1)),
            dma((REACH - 1, NC)),
            dma((REACH - 1, NC)),
        ],
        compiler_params=pltpu.CompilerParams(
            collective_id=1, has_side_effects=True, vmem_limit_bytes=32 * 2**20
        ),
        name="multiply_scatter",
    )(fit)


def body(near, blocks, slot_rows, slot_shells, shell_order, support, coeffs):
    gathered = gather_coeffs(coeffs) if near else lax.all_gather(coeffs, "aux", axis=0, tiled=True)
    fit = fit_rows(shell_order, support.T, slot_rows, slot_shells, gathered, blocks)
    if near:
        return multiply_scatter(fit)
    product = lax.dot_general(fit, fit, (((0,), (0,)), ((), ())), preferred_element_type=jnp.float32)
    return lax.psum_scatter(product, "aux", scatter_dimension=0, tiled=True)


def solution(mesh):
    return jax.shard_map(
        functools.partial(body, mesh.shape["aux"] == NZ * NX * NC),
        mesh=mesh,
        in_specs=(
            P(("frag", "aux"), None, None),
            P(("frag", "aux")),
            P(("frag", "aux")),
            P("frag"),
            P("frag", None),
            P(("frag", "aux"), None, None),
        ),
        out_specs=P(("frag", "aux"), None),
        check_vma=False,
    )
```

```python
import functools

import jax
import jax.numpy as jnp
from jax import lax
from jax.experimental import pallas as pl
from jax.experimental.pallas import tpu as pltpu
from jax.sharding import PartitionSpec as P

NOB = 16
ROWS = 16
NZ, NX, NC = 4, 2, 2
CHIPS = NZ * NX
REACH = CHIPS // 2


def device(z, x, c):
    return {"aux": (z * NX + x) * NC + c}


def here():
    me = lax.axis_index("aux")
    return me // (NX * NC), (me // NC) % NX, me % NC


def gather_kernel(own, out, local, z_recv, x_recv, m_recv, r_send, l_send, x_send, m_send):
    z, x, c = here()
    mate, across = device(z, x, 1 - c), device(z, 1 - x, c)

    keep = pltpu.make_async_copy(own, out.at[(z * NX + x) * NC + c], local)
    keep.start()
    barrier = pltpu.get_barrier_semaphore()
    pl.semaphore_signal(barrier, inc=1, device_id=mate)
    pl.semaphore_signal(barrier, inc=1, device_id=across)

    @pl.when(z > 0)
    def _():
        pl.semaphore_signal(barrier, inc=1, device_id=device(z - 1, x, c))

    @pl.when(z < NZ - 1)
    def _():
        pl.semaphore_signal(barrier, inc=1, device_id=device(z + 1, x, c))

    pl.semaphore_wait(barrier, 2 + jnp.where(z > 0, 1, 0) + jnp.where(z < NZ - 1, 1, 0))

    def copy(zz, xx, to, send, recv, first=False):
        spot = out.at[(zz * NX + xx) * NC + c]
        return pltpu.make_async_remote_copy(
            src_ref=own if first else spot, dst_ref=spot, send_sem=send, recv_sem=recv, device_id=to
        )

    def to_right(zz, first=False):
        return copy(zz, x, device(z + 1, x, c), r_send.at[zz], z_recv.at[zz], first)

    def to_left(zz, first=False):
        return copy(zz, x, device(z - 1, x, c), l_send.at[zz], z_recv.at[zz], first)

    def to_across(zz, first=False):
        return copy(zz, x, across, x_send.at[zz], x_recv.at[zz], first)

    def to_mate(zz, xx, first=False):
        spot = xx * NZ + zz
        return copy(zz, xx, mate, m_send.at[spot], m_recv.at[spot], first)

    def arrived_across(zz):
        pltpu.make_async_remote_copy(
            src_ref=own,
            dst_ref=out.at[(zz * NX + 1 - x) * NC + c],
            send_sem=x_send.at[zz],
            recv_sem=x_recv.at[zz],
            device_id=across,
        ).wait_recv()
        to_mate(zz, 1 - x).start()

    @pl.when(z < NZ - 1)
    def _():
        to_right(z, True).start()

    @pl.when(z > 0)
    def _():
        to_left(z, True).start()

    to_across(z, True).start()
    to_mate(z, x, True).start()
    for step in range(1, NZ):

        @pl.when(z - step >= 0)
        def _():
            zz = z - step
            copy(zz, x, across, r_send.at[zz], z_recv.at[zz]).wait_recv()

            @pl.when(z < NZ - 1)
            def _():
                to_right(zz).start()

            to_across(zz).start()
            to_mate(zz, x).start()

        @pl.when(z + step < NZ)
        def _():
            zz = z + step
            copy(zz, x, across, l_send.at[zz], z_recv.at[zz]).wait_recv()

            @pl.when(z > 0)
            def _():
                to_left(zz).start()

            to_across(zz).start()
            to_mate(zz, x).start()

        if step == 1:
            arrived_across(z)

    for step in range(1, NZ):

        @pl.when(z - step >= 0)
        def _():
            arrived_across(z - step)

        @pl.when(z + step < NZ)
        def _():
            arrived_across(z + step)

    keep.wait()
    for zz in range(NZ):

        @pl.when((zz <= z) & (z < NZ - 1))
        def _():
            to_right(zz).wait_send()

        @pl.when((zz >= z) & (z > 0))
        def _():
            to_left(zz).wait_send()

        to_across(zz).wait_send()
        for xx in range(NX):
            to_mate(zz, xx).wait_send()
            pltpu.make_async_remote_copy(
                src_ref=own,
                dst_ref=out.at[(zz * NX + xx) * NC + 1 - c],
                send_sem=m_send.at[xx * NZ + zz],
                recv_sem=m_recv.at[xx * NZ + zz],
                device_id=mate,
            ).wait_recv()


def gather_coeffs(coeffs):
    count = NZ * NX * NC
    dma = pltpu.SemaphoreType.DMA
    out = pl.pallas_call(
        gather_kernel,
        out_shape=jax.ShapeDtypeStruct((count,) + coeffs.shape, coeffs.dtype),
        in_specs=[pl.BlockSpec(memory_space=pl.ANY)],
        out_specs=pl.BlockSpec(memory_space=pl.ANY),
        scratch_shapes=[
            dma,
            dma((NZ,)),
            dma((NZ,)),
            dma((CHIPS,)),
            dma((NZ,)),
            dma((NZ,)),
            dma((NZ,)),
            dma((CHIPS,)),
        ],
        compiler_params=pltpu.CompilerParams(collective_id=0, has_side_effects=True),
        name="gather_coeffs",
    )(coeffs)
    return out.reshape((count * coeffs.shape[0],) + coeffs.shape[1:])


def fit_kernel(order, supp, rows, shells, gathered, blocks, fit, inv, acc, coef, loaded):
    load = pltpu.make_async_copy(gathered, coef, loaded)
    load.start()
    shell_total = order.shape[0]
    slot_count, size, width = blocks.shape
    supp_count = supp.shape[0]
    orb = coef.shape[2] // supp_count
    tiles = fit.shape[1] // width
    depth = NOB * orb

    def invert(k, carry):
        inv[order[k]] = k
        return carry

    lax.fori_loop(0, shell_total, invert, 0, unroll=8)

    def clear(k, carry):
        acc[k] = jnp.zeros(acc.shape[1:], jnp.float32)
        return carry

    lax.fori_loop(0, ROWS * NOB, clear, 0, unroll=4)
    load.wait()

    batch = 8 if slot_count % 8 == 0 else 1

    def slots(n, carry):
        halves = []
        for s in range(batch):
            shell = shells[n * batch + s]
            half = lax.dot_general(
                coef[inv[shell]],
                blocks[n * batch + s],
                (((0,), (0,)), ((), ())),
                preferred_element_type=jnp.float32,
            )
            halves.append(half.astype(jnp.bfloat16).astype(jnp.float32))
        for s, half in enumerate(halves):
            shell = shells[n * batch + s]
            row = rows[n * batch + s]
            for a in range(supp_count):
                spot = row * NOB + supp[a, shell]
                acc[spot] = acc[spot] + half[a * orb : (a + 1) * orb]
        return carry

    lax.fori_loop(0, slot_count // batch, slots, 0, unroll=2)

    low = lax.broadcasted_iota(jnp.int32, (orb, width), 1) < size

    def regroup(b, carry):
        for j in range(tiles):
            even = acc[2 * j * NOB + b]
            odd = acc[(2 * j + 1) * NOB + b]
            first = jnp.where(low, even, pltpu.roll(odd, size, 1)).astype(jnp.bfloat16)
            second = jnp.where(low, pltpu.roll(even, size, 1), odd).astype(jnp.bfloat16)
            cut = slice(j * width, (j + 1) * width)
            fit[pl.ds(pl.multiple_of(b * orb, orb), orb), cut] = first
            fit[pl.ds(pl.multiple_of(depth + b * orb, orb), orb), cut] = second
        return carry

    lax.fori_loop(0, NOB, regroup, 0)


def fit_rows(order, supp, rows, shells, coef, blocks):
    size, width = blocks.shape[1:]
    orb = coef.shape[2] // supp.shape[0]
    smem = pl.BlockSpec(memory_space=pltpu.SMEM)
    vmem = pl.BlockSpec(memory_space=pltpu.VMEM)
    return pl.pallas_call(
        fit_kernel,
        out_shape=jax.ShapeDtypeStruct((NOB * orb * width // size, ROWS * size), jnp.bfloat16),
        in_specs=[smem] * 4 + [pl.BlockSpec(memory_space=pl.ANY), vmem],
        out_specs=vmem,
        scratch_shapes=[
            pltpu.SMEM(order.shape, jnp.int32),
            pltpu.VMEM((ROWS * NOB, orb, width), jnp.float32),
            pltpu.VMEM(coef.shape, coef.dtype),
            pltpu.SemaphoreType.DMA,
        ],
        compiler_params=pltpu.CompilerParams(vmem_limit_bytes=46 * 2**20),
        name="fit_rows",
    )(order, supp, rows, shells, coef, blocks)


def scatter_kernel(
    fit, out, held, part, from_mate, mine_a, mine_b, across_a, across_b, line_a, line_b, mirror, total,
    local, m_send, m_recv, x_send, x_recv, z_send, z_recv, t_send, t_recv,
):
    z, x, c = here()
    chip = z * NX + x
    mate, across = device(z, x, 1 - c), device(z, 1 - x, c)
    full = fit.shape[1]
    lanes = mirror.shape[3]
    rows, window = from_mate.shape[1:]
    mine, from_across, from_line = (mine_a, mine_b), (across_a, across_b), (line_a, line_b)

    keeps = [
        pltpu.make_async_copy(fit, held.at[:, :full], local.at[0]),
        pltpu.make_async_copy(
            fit.at[:, : window - lanes], held.at[:, full : full + window - lanes], local.at[1]
        ),
    ]
    for keep in keeps:
        keep.start()

    barrier = pltpu.get_barrier_semaphore()
    me = lax.axis_index("aux")
    count = CHIPS * NC
    for step in range(1, count):
        pl.semaphore_signal(barrier, inc=1, device_id={"aux": lax.rem(me + step, count)})
    for keep in keeps:
        keep.wait()
    pl.semaphore_wait(barrier, count - 1)

    def send(src, dst, to, send_sem, recv_sem):
        copy = pltpu.make_async_remote_copy(
            src_ref=src, dst_ref=dst, send_sem=send_sem, recv_sem=recv_sem, device_id=to
        )
        copy.start()
        return copy

    own_rows = pl.ds(pl.multiple_of(c * rows, rows), rows)
    mate_rows = pl.ds(pl.multiple_of((1 - c) * rows, rows), rows)

    def to_mate(j):
        return pltpu.make_async_remote_copy(
            src_ref=part.at[j, mate_rows],
            dst_ref=from_mate.at[j],
            send_sem=m_send.at[j],
            recv_sem=m_recv.at[j],
            device_id=mate,
        )

    def to_across(g, j):
        return pltpu.make_async_remote_copy(
            src_ref=mine[g].at[j],
            dst_ref=from_across[g].at[j],
            send_sem=x_send.at[g, j],
            recv_sem=x_recv.at[g, j],
            device_id=across,
        )

    def add_pair(j):
        to_mate(j).wait_recv()
        both = part[j, own_rows] + from_mate[j]
        mine_a[j] = both[:, lanes : REACH * lanes]
        mine_b[j, :, :lanes] = both[:, :lanes]
        mine_b[j, :, lanes:] = both[:, REACH * lanes :]

    def packet(j, carry):
        column = jnp.where(j < NZ, 1 - x, x)
        start = pl.multiple_of((lax.rem(z + 1 + j, NZ) * NX + column) * lanes, lanes)
        part[j] = lax.dot_general(
            held[:, pl.ds(start, lanes)],
            held[:, pl.ds(start, window)],
            (((0,), (0,)), ((), ())),
            preferred_element_type=jnp.float32,
        )
        to_mate(j).start()

        @pl.when((j >= 1) & (j <= NZ))
        def _():
            add_pair(j - 1)
            to_across(0, j - 1).start()

        return carry

    lax.fori_loop(0, CHIPS, packet, 0)
    to_line = []

    def pass_on(g, j):
        k = NZ + j
        to_across(g, j).wait_recv()
        mine[g][k] = mine[g][k] + from_across[g][j]
        if j < NZ - 1:
            to_line.append(
                send(
                    mine[g].at[k],
                    from_line[g].at[j],
                    device(lax.rem(z + 1 + j, NZ), x, c),
                    z_send.at[g, j],
                    z_recv.at[g, j],
                )
            )

    def finish(g, blocks):
        for copy in to_line[g * (NZ - 1) : (g + 1) * (NZ - 1)]:
            copy.wait_recv()
        for at, k in enumerate(blocks):
            cut = slice(at * lanes, (at + 1) * lanes)
            summed = mine[g][CHIPS - 1, :, cut]
            for j in range(NZ - 1):
                summed = summed + from_line[g][j, :, cut]
            total[k] = summed

    for j in range(NZ):
        add_pair(NZ + j)
    for j in range(NZ):
        pass_on(0, j)
        to_across(1, j).start()
    pass_on(1, 0)
    pass_on(1, 1)
    finish(0, range(1, REACH))
    to_mirror = []
    for k in range(1, REACH):
        for e in range(NC):
            to_mirror.append(
                send(
                    total.at[k],
                    mirror.at[k - 1, c],
                    {"aux": lax.rem(chip + k, CHIPS) * NC + e},
                    t_send.at[k - 1, e],
                    t_recv.at[k - 1, c],
                )
            )
    for j in range(2, NZ):
        pass_on(1, j)
    finish(1, (0, REACH))
    for k in range(REACH + 1):
        at = pl.multiple_of(lax.rem(chip + k, CHIPS) * lanes, lanes)
        out[:, pl.ds(at, lanes)] = total[k]
    for k in range(1, REACH):
        for e in range(NC):
            pltpu.make_async_remote_copy(
                src_ref=total.at[k],
                dst_ref=mirror.at[k - 1, e],
                send_sem=t_send.at[k - 1, e],
                recv_sem=t_recv.at[k - 1, e],
                device_id=mate,
            ).wait_recv()
        turned = mirror[k - 1].reshape(NC * rows, lanes).T
        at = pl.multiple_of(lax.rem(chip + CHIPS - k, CHIPS) * lanes, lanes)
        out[:, pl.ds(at, lanes)] = jnp.where(c == 0, turned[:rows], turned[rows:])
    for j in range(CHIPS):
        to_mate(j).wait_send()
    for g in range(2):
        for j in range(NZ):
            to_across(g, j).wait_send()
    for copy in to_line + to_mirror:
        copy.wait_send()


def multiply_scatter(fit):
    depth, full = fit.shape
    lanes = full // CHIPS
    rows, window = lanes // NC, (REACH + 1) * lanes
    first = (REACH - 1) * lanes
    dma = pltpu.SemaphoreType.DMA
    return pl.pallas_call(
        scatter_kernel,
        out_shape=jax.ShapeDtypeStruct((rows, full), jnp.float32),
        in_specs=[pl.BlockSpec(memory_space=pl.ANY)],
        out_specs=pl.BlockSpec(memory_space=pltpu.VMEM),
        scratch_shapes=[
            pltpu.VMEM((depth, full + window - lanes), jnp.bfloat16),
            pltpu.VMEM((CHIPS, lanes, window), jnp.float32),
            pltpu.VMEM((CHIPS, rows, window), jnp.float32),
            pltpu.VMEM((CHIPS, rows, first), jnp.float32),
            pltpu.VMEM((CHIPS, rows, window - first), jnp.float32),
            pltpu.VMEM((NZ, rows, first), jnp.float32),
            pltpu.VMEM((NZ, rows, window - first), jnp.float32),
            pltpu.VMEM((NZ - 1, rows, first), jnp.float32),
            pltpu.VMEM((NZ - 1, rows, window - first), jnp.float32),
            pltpu.VMEM((REACH - 1, NC, rows, lanes), jnp.float32),
            pltpu.VMEM((REACH + 1, rows, lanes), jnp.float32),
            dma((2,)),
            dma((CHIPS,)),
            dma((CHIPS,)),
            dma((2, NZ)),
            dma((2, NZ)),
            dma((2, NZ - 1)),
            dma((2, NZ - 1)),
            dma((REACH - 1, NC)),
            dma((REACH - 1, NC)),
        ],
        compiler_params=pltpu.CompilerParams(
            collective_id=1, has_side_effects=True, vmem_limit_bytes=32 * 2**20
        ),
        name="multiply_scatter",
    )(fit)


def body(near, blocks, slot_rows, slot_shells, shell_order, support, coeffs):
    gathered = gather_coeffs(coeffs) if near else lax.all_gather(coeffs, "aux", axis=0, tiled=True)
    fit = fit_rows(shell_order, support.T, slot_rows, slot_shells, gathered, blocks)
    if near:
        return multiply_scatter(fit)
    product = lax.dot_general(fit, fit, (((0,), (0,)), ((), ())), preferred_element_type=jnp.float32)
    return lax.psum_scatter(product, "aux", scatter_dimension=0, tiled=True)


def solution(mesh):
    return jax.shard_map(
        functools.partial(body, mesh.shape["aux"] == NZ * NX * NC),
        mesh=mesh,
        in_specs=(
            P(("frag", "aux"), None, None),
            P(("frag", "aux")),
            P(("frag", "aux")),
            P("frag"),
            P("frag", None),
            P(("frag", "aux"), None, None),
        ),
        out_specs=P(("frag", "aux"), None),
        check_vma=False,
    )
```

```python
import functools

import jax
import jax.numpy as jnp
from jax import lax
from jax.experimental import pallas as pl
from jax.experimental.pallas import tpu as pltpu
from jax.sharding import PartitionSpec as P

NOB = 16
ROWS = 16
NZ, NX, NC = 4, 2, 2
CHIPS = NZ * NX
REACH = CHIPS // 2


def device(z, x, c):
    return {"aux": (z * NX + x) * NC + c}


def here():
    me = lax.axis_index("aux")
    return me // (NX * NC), (me // NC) % NX, me % NC


def gather_kernel(
    whole, full_out, local, z_recv, x_recv, m_recv, r_send, l_send, x_send, m_send,
    bz_recv, bx_recv, bm_recv, br_send, bl_send, bx_send, bm_send,
):
    held = whole.shape[0]
    cut = held - held // 8
    own, out = whole.at[:cut], full_out.at[:, :cut]
    b_own, b_out = whole.at[cut:], full_out.at[:, cut:]
    z, x, c = here()
    mate, across = device(z, x, 1 - c), device(z, 1 - x, c)

    keep = pltpu.make_async_copy(whole, full_out.at[(z * NX + x) * NC + c], local)
    keep.start()
    barrier = pltpu.get_barrier_semaphore()
    pl.semaphore_signal(barrier, inc=1, device_id=mate)
    pl.semaphore_signal(barrier, inc=1, device_id=across)

    @pl.when(z > 0)
    def _():
        pl.semaphore_signal(barrier, inc=1, device_id=device(z - 1, x, c))

    @pl.when(z < NZ - 1)
    def _():
        pl.semaphore_signal(barrier, inc=1, device_id=device(z + 1, x, c))

    pl.semaphore_wait(barrier, 2 + jnp.where(z > 0, 1, 0) + jnp.where(z < NZ - 1, 1, 0))

    def copy(zz, xx, to, send, recv, first=False):
        spot = out.at[(zz * NX + xx) * NC + c]
        return pltpu.make_async_remote_copy(
            src_ref=own if first else spot, dst_ref=spot, send_sem=send, recv_sem=recv, device_id=to
        )

    def to_right(zz, first=False):
        return copy(zz, x, device(z + 1, x, c), r_send.at[zz], z_recv.at[zz], first)

    def to_left(zz, first=False):
        return copy(zz, x, device(z - 1, x, c), l_send.at[zz], z_recv.at[zz], first)

    def to_across(zz, first=False):
        return copy(zz, x, across, x_send.at[zz], x_recv.at[zz], first)

    def to_mate(zz, xx, first=False):
        spot = xx * NZ + zz
        return copy(zz, xx, mate, m_send.at[spot], m_recv.at[spot], first)

    def arrived_across(zz):
        pltpu.make_async_remote_copy(
            src_ref=own,
            dst_ref=out.at[(zz * NX + 1 - x) * NC + c],
            send_sem=x_send.at[zz],
            recv_sem=x_recv.at[zz],
            device_id=across,
        ).wait_recv()
        to_mate(zz, 1 - x).start()

    def b_copy(zz, xx, to, send, recv, first=False):
        spot = b_out.at[(zz * NX + xx) * NC + c]
        return pltpu.make_async_remote_copy(
            src_ref=b_own if first else spot, dst_ref=spot, send_sem=send, recv_sem=recv, device_id=to
        )

    def b_right(zz, xx, first=False):
        return b_copy(zz, xx, device(z + 1, x, c), br_send.at[zz, xx], bz_recv.at[zz, xx], first)

    def b_left(zz, xx, first=False):
        return b_copy(zz, xx, device(z - 1, x, c), bl_send.at[zz, xx], bz_recv.at[zz, xx], first)

    def b_mate(zz, xx, first=False):
        return b_copy(zz, xx, mate, bm_send.at[zz, xx], bm_recv.at[zz, xx], first)

    def b_spread(xx, first):
        @pl.when(z < NZ - 1)
        def _():
            b_right(z, xx, first).start()

        @pl.when(z > 0)
        def _():
            b_left(z, xx, first).start()

        b_mate(z, xx, first).start()

    b_across = b_copy(z, x, across, bx_send, bx_recv, True)
    b_across.start()
    b_spread(x, True)

    @pl.when(z < NZ - 1)
    def _():
        to_right(z, True).start()

    @pl.when(z > 0)
    def _():
        to_left(z, True).start()

    to_across(z, True).start()
    to_mate(z, x, True).start()
    b_copy(z, 1 - x, across, bx_send, bx_recv).wait_recv()
    b_spread(1 - x, False)
    for step in range(1, NZ):

        @pl.when(z - step >= 0)
        def _():
            zz = z - step
            for xx in range(NX):
                b_copy(zz, xx, across, br_send.at[zz, xx], bz_recv.at[zz, xx]).wait_recv()

                @pl.when(z < NZ - 1)
                def _():
                    b_right(zz, xx).start()

                b_mate(zz, xx).start()
            copy(zz, x, across, r_send.at[zz], z_recv.at[zz]).wait_recv()

            @pl.when(z < NZ - 1)
            def _():
                to_right(zz).start()

            to_across(zz).start()
            to_mate(zz, x).start()

        @pl.when(z + step < NZ)
        def _():
            zz = z + step
            for xx in range(NX):
                b_copy(zz, xx, across, bl_send.at[zz, xx], bz_recv.at[zz, xx]).wait_recv()

                @pl.when(z > 0)
                def _():
                    b_left(zz, xx).start()

                b_mate(zz, xx).start()
            copy(zz, x, across, l_send.at[zz], z_recv.at[zz]).wait_recv()

            @pl.when(z > 0)
            def _():
                to_left(zz).start()

            to_across(zz).start()
            to_mate(zz, x).start()

        if step == 1:
            arrived_across(z)

    for step in range(1, NZ):

        @pl.when(z - step >= 0)
        def _():
            arrived_across(z - step)

        @pl.when(z + step < NZ)
        def _():
            arrived_across(z + step)

    keep.wait()
    b_across.wait_send()
    for zz in range(NZ):
        for xx in range(NX):

            @pl.when((zz <= z) & (z < NZ - 1))
            def _():
                b_right(zz, xx).wait_send()

            @pl.when((zz >= z) & (z > 0))
            def _():
                b_left(zz, xx).wait_send()

            b_mate(zz, xx).wait_send()
            pltpu.make_async_remote_copy(
                src_ref=b_own,
                dst_ref=b_out.at[(zz * NX + xx) * NC + 1 - c],
                send_sem=bm_send.at[zz, xx],
                recv_sem=bm_recv.at[zz, xx],
                device_id=mate,
            ).wait_recv()

        @pl.when((zz <= z) & (z < NZ - 1))
        def _():
            to_right(zz).wait_send()

        @pl.when((zz >= z) & (z > 0))
        def _():
            to_left(zz).wait_send()

        to_across(zz).wait_send()
        for xx in range(NX):
            to_mate(zz, xx).wait_send()
            pltpu.make_async_remote_copy(
                src_ref=own,
                dst_ref=out.at[(zz * NX + xx) * NC + 1 - c],
                send_sem=m_send.at[xx * NZ + zz],
                recv_sem=m_recv.at[xx * NZ + zz],
                device_id=mate,
            ).wait_recv()


def gather_coeffs(coeffs):
    count = NZ * NX * NC
    dma = pltpu.SemaphoreType.DMA
    out = pl.pallas_call(
        gather_kernel,
        out_shape=jax.ShapeDtypeStruct((count,) + coeffs.shape, coeffs.dtype),
        in_specs=[pl.BlockSpec(memory_space=pl.ANY)],
        out_specs=pl.BlockSpec(memory_space=pl.ANY),
        scratch_shapes=[
            dma,
            dma((NZ,)),
            dma((NZ,)),
            dma((CHIPS,)),
            dma((NZ,)),
            dma((NZ,)),
            dma((NZ,)),
            dma((CHIPS,)),
            dma((NZ, NX)),
            dma,
            dma((NZ, NX)),
            dma((NZ, NX)),
            dma((NZ, NX)),
            dma,
            dma((NZ, NX)),
        ],
        compiler_params=pltpu.CompilerParams(collective_id=0, has_side_effects=True),
        name="gather_coeffs",
    )(coeffs)
    return out.reshape((count * coeffs.shape[0],) + coeffs.shape[1:])


def fit_kernel(order, supp, rows, shells, gathered, blocks, fit, inv, acc, coef, loaded):
    load = pltpu.make_async_copy(gathered, coef, loaded)
    load.start()
    shell_total = order.shape[0]
    slot_count, size, width = blocks.shape
    supp_count = supp.shape[0]
    orb = coef.shape[2] // supp_count
    tiles = fit.shape[1] // width
    depth = NOB * orb

    def invert(k, carry):
        inv[order[k]] = k
        return carry

    lax.fori_loop(0, shell_total, invert, 0, unroll=8)

    def clear(k, carry):
        acc[k] = jnp.zeros(acc.shape[1:], jnp.float32)
        return carry

    lax.fori_loop(0, ROWS * NOB, clear, 0, unroll=4)
    load.wait()

    batch = 8 if slot_count % 8 == 0 else 1

    def slots(n, carry):
        halves = []
        for s in range(batch):
            shell = shells[n * batch + s]
            half = lax.dot_general(
                coef[inv[shell]],
                blocks[n * batch + s],
                (((0,), (0,)), ((), ())),
                preferred_element_type=jnp.float32,
            )
            halves.append(half.astype(jnp.bfloat16).astype(jnp.float32))
        for s, half in enumerate(halves):
            shell = shells[n * batch + s]
            row = rows[n * batch + s]
            for a in range(supp_count):
                spot = row * NOB + supp[a, shell]
                acc[spot] = acc[spot] + half[a * orb : (a + 1) * orb]
        return carry

    lax.fori_loop(0, slot_count // batch, slots, 0, unroll=2)

    low = lax.broadcasted_iota(jnp.int32, (orb, width), 1) < size

    def regroup(b, carry):
        for j in range(tiles):
            even = acc[2 * j * NOB + b]
            odd = acc[(2 * j + 1) * NOB + b]
            first = jnp.where(low, even, pltpu.roll(odd, size, 1)).astype(jnp.bfloat16)
            second = jnp.where(low, pltpu.roll(even, size, 1), odd).astype(jnp.bfloat16)
            cut = slice(j * width, (j + 1) * width)
            fit[pl.ds(pl.multiple_of(b * orb, orb), orb), cut] = first
            fit[pl.ds(pl.multiple_of(depth + b * orb, orb), orb), cut] = second
        return carry

    lax.fori_loop(0, NOB, regroup, 0)


def fit_rows(order, supp, rows, shells, coef, blocks):
    size, width = blocks.shape[1:]
    orb = coef.shape[2] // supp.shape[0]
    smem = pl.BlockSpec(memory_space=pltpu.SMEM)
    vmem = pl.BlockSpec(memory_space=pltpu.VMEM)
    return pl.pallas_call(
        fit_kernel,
        out_shape=jax.ShapeDtypeStruct((NOB * orb * width // size, ROWS * size), jnp.bfloat16),
        in_specs=[smem] * 4 + [pl.BlockSpec(memory_space=pl.ANY), vmem],
        out_specs=vmem,
        scratch_shapes=[
            pltpu.SMEM(order.shape, jnp.int32),
            pltpu.VMEM((ROWS * NOB, orb, width), jnp.float32),
            pltpu.VMEM(coef.shape, coef.dtype),
            pltpu.SemaphoreType.DMA,
        ],
        compiler_params=pltpu.CompilerParams(vmem_limit_bytes=46 * 2**20),
        name="fit_rows",
    )(order, supp, rows, shells, coef, blocks)


def scatter_kernel(
    fit, out, held, part, from_mate, mine_a, mine_b, across_a, across_b, line_a, line_b, mirror, total,
    local, m_send, m_recv, x_send, x_recv, z_send, z_recv, t_send, t_recv,
):
    z, x, c = here()
    chip = z * NX + x
    mate, across = device(z, x, 1 - c), device(z, 1 - x, c)
    full = fit.shape[1]
    lanes = mirror.shape[3]
    rows, window = from_mate.shape[1:]
    mine, from_across, from_line = (mine_a, mine_b), (across_a, across_b), (line_a, line_b)

    keeps = [
        pltpu.make_async_copy(fit, held.at[:, :full], local.at[0]),
        pltpu.make_async_copy(
            fit.at[:, : window - lanes], held.at[:, full : full + window - lanes], local.at[1]
        ),
    ]
    for keep in keeps:
        keep.start()

    barrier = pltpu.get_barrier_semaphore()
    me = lax.axis_index("aux")
    count = CHIPS * NC
    for step in range(1, count):
        pl.semaphore_signal(barrier, inc=1, device_id={"aux": lax.rem(me + step, count)})
    for keep in keeps:
        keep.wait()
    pl.semaphore_wait(barrier, count - 1)

    def send(src, dst, to, send_sem, recv_sem):
        copy = pltpu.make_async_remote_copy(
            src_ref=src, dst_ref=dst, send_sem=send_sem, recv_sem=recv_sem, device_id=to
        )
        copy.start()
        return copy

    own_rows = pl.ds(pl.multiple_of(c * rows, rows), rows)
    mate_rows = pl.ds(pl.multiple_of((1 - c) * rows, rows), rows)

    def to_mate(j):
        return pltpu.make_async_remote_copy(
            src_ref=part.at[j, mate_rows],
            dst_ref=from_mate.at[j],
            send_sem=m_send.at[j],
            recv_sem=m_recv.at[j],
            device_id=mate,
        )

    def to_across(g, j):
        return pltpu.make_async_remote_copy(
            src_ref=mine[g].at[j],
            dst_ref=from_across[g].at[j],
            send_sem=x_send.at[g, j],
            recv_sem=x_recv.at[g, j],
            device_id=across,
        )

    def add_pair(j):
        to_mate(j).wait_recv()
        both = part[j, own_rows] + from_mate[j]
        mine_a[j] = both[:, lanes : REACH * lanes]
        mine_b[j, :, :lanes] = both[:, :lanes]
        mine_b[j, :, lanes:] = both[:, REACH * lanes :]

    def packet(j, carry):
        column = jnp.where(j < NZ, 1 - x, x)
        start = pl.multiple_of((lax.rem(z + 1 + j, NZ) * NX + column) * lanes, lanes)
        part[j] = lax.dot_general(
            held[:, pl.ds(start, lanes)],
            held[:, pl.ds(start, window)],
            (((0,), (0,)), ((), ())),
            preferred_element_type=jnp.float32,
        )
        to_mate(j).start()

        @pl.when((j >= 1) & (j <= NZ))
        def _():
            add_pair(j - 1)
            to_across(0, j - 1).start()

        return carry

    lax.fori_loop(0, CHIPS, packet, 0)
    to_line = []

    def pass_on(g, j):
        k = NZ + j
        to_across(g, j).wait_recv()
        mine[g][k] = mine[g][k] + from_across[g][j]
        if j < NZ - 1:
            to_line.append(
                send(
                    mine[g].at[k],
                    from_line[g].at[j],
                    device(lax.rem(z + 1 + j, NZ), x, c),
                    z_send.at[g, j],
                    z_recv.at[g, j],
                )
            )

    def finish(g, blocks):
        for copy in to_line[g * (NZ - 1) : (g + 1) * (NZ - 1)]:
            copy.wait_recv()
        for at, k in enumerate(blocks):
            cut = slice(at * lanes, (at + 1) * lanes)
            summed = mine[g][CHIPS - 1, :, cut]
            for j in range(NZ - 1):
                summed = summed + from_line[g][j, :, cut]
            total[k] = summed

    for j in range(NZ):
        add_pair(NZ + j)
    for j in range(NZ):
        pass_on(0, j)
        to_across(1, j).start()
    pass_on(1, 0)
    pass_on(1, 1)
    finish(0, range(1, REACH))
    to_mirror = []
    for k in range(1, REACH):
        for e in range(NC):
            to_mirror.append(
                send(
                    total.at[k],
                    mirror.at[k - 1, c],
                    {"aux": lax.rem(chip + k, CHIPS) * NC + e},
                    t_send.at[k - 1, e],
                    t_recv.at[k - 1, c],
                )
            )
    for j in range(2, NZ):
        pass_on(1, j)
    finish(1, (0, REACH))
    for k in range(REACH + 1):
        at = pl.multiple_of(lax.rem(chip + k, CHIPS) * lanes, lanes)
        out[:, pl.ds(at, lanes)] = total[k]
    for k in range(1, REACH):
        for e in range(NC):
            pltpu.make_async_remote_copy(
                src_ref=total.at[k],
                dst_ref=mirror.at[k - 1, e],
                send_sem=t_send.at[k - 1, e],
                recv_sem=t_recv.at[k - 1, e],
                device_id=mate,
            ).wait_recv()
        turned = mirror[k - 1].reshape(NC * rows, lanes).T
        at = pl.multiple_of(lax.rem(chip + CHIPS - k, CHIPS) * lanes, lanes)
        out[:, pl.ds(at, lanes)] = jnp.where(c == 0, turned[:rows], turned[rows:])
    for j in range(CHIPS):
        to_mate(j).wait_send()
    for g in range(2):
        for j in range(NZ):
            to_across(g, j).wait_send()
    for copy in to_line + to_mirror:
        copy.wait_send()


def multiply_scatter(fit):
    depth, full = fit.shape
    lanes = full // CHIPS
    rows, window = lanes // NC, (REACH + 1) * lanes
    first = (REACH - 1) * lanes
    dma = pltpu.SemaphoreType.DMA
    return pl.pallas_call(
        scatter_kernel,
        out_shape=jax.ShapeDtypeStruct((rows, full), jnp.float32),
        in_specs=[pl.BlockSpec(memory_space=pl.ANY)],
        out_specs=pl.BlockSpec(memory_space=pltpu.VMEM),
        scratch_shapes=[
            pltpu.VMEM((depth, full + window - lanes), jnp.bfloat16),
            pltpu.VMEM((CHIPS, lanes, window), jnp.float32),
            pltpu.VMEM((CHIPS, rows, window), jnp.float32),
            pltpu.VMEM((CHIPS, rows, first), jnp.float32),
            pltpu.VMEM((CHIPS, rows, window - first), jnp.float32),
            pltpu.VMEM((NZ, rows, first), jnp.float32),
            pltpu.VMEM((NZ, rows, window - first), jnp.float32),
            pltpu.VMEM((NZ - 1, rows, first), jnp.float32),
            pltpu.VMEM((NZ - 1, rows, window - first), jnp.float32),
            pltpu.VMEM((REACH - 1, NC, rows, lanes), jnp.float32),
            pltpu.VMEM((REACH + 1, rows, lanes), jnp.float32),
            dma((2,)),
            dma((CHIPS,)),
            dma((CHIPS,)),
            dma((2, NZ)),
            dma((2, NZ)),
            dma((2, NZ - 1)),
            dma((2, NZ - 1)),
            dma((REACH - 1, NC)),
            dma((REACH - 1, NC)),
        ],
        compiler_params=pltpu.CompilerParams(
            collective_id=1, has_side_effects=True, vmem_limit_bytes=32 * 2**20
        ),
        name="multiply_scatter",
    )(fit)


def body(near, blocks, slot_rows, slot_shells, shell_order, support, coeffs):
    gathered = gather_coeffs(coeffs) if near else lax.all_gather(coeffs, "aux", axis=0, tiled=True)
    fit = fit_rows(shell_order, support.T, slot_rows, slot_shells, gathered, blocks)
    if near:
        return multiply_scatter(fit)
    product = lax.dot_general(fit, fit, (((0,), (0,)), ((), ())), preferred_element_type=jnp.float32)
    return lax.psum_scatter(product, "aux", scatter_dimension=0, tiled=True)


def solution(mesh):
    return jax.shard_map(
        functools.partial(body, mesh.shape["aux"] == NZ * NX * NC),
        mesh=mesh,
        in_specs=(
            P(("frag", "aux"), None, None),
            P(("frag", "aux")),
            P(("frag", "aux")),
            P("frag"),
            P("frag", None),
            P(("frag", "aux"), None, None),
        ),
        out_specs=P(("frag", "aux"), None),
        check_vma=False,
    )
```
